512 devices in a mesh: pts: 64 (over y, z), tgt: 8 (over x, core).
Axes of the slice: x: 4, y: 4, z: 16, core: 2. Of those that a mesh axis runs over, the one named last changes fastest.
Arguments:
- template_points: float32 [3, 98304], P(None, 'pts'), may hold values from 0 to 24
- template_mass: float32 [98304], P('pts'), may hold values from 0.5 to 2
- target_points: float32 [32, 3, 98304], P('tgt', None, 'pts'), may hold values from 0 to 24
- target_mass: float32 [32, 98304], P('tgt', 'pts'), may hold values from 0.5 to 2
- pattern: int32 [32, 768, 4], P('tgt', 'pts'), may hold values from 0 to 767, as said below
Outputs:
- position_grad: float32 [3, 98304], P(None, 'pts')
- target_potentials: float32 [32, 98304], P('tgt', 'pts')
The draws below stay inside these ranges and needn't reach their ends.
Inputs may be any that keep to these rules, and one draw needn't show every extreme that they name: pattern[t, p, 0] is p; the other 3 entries of pattern[t, p, :] are distinct, differ from p, and name target blocks q with |q - p| <= 12.
All inputs are finite; a program needn't handle non-finite values.
Results may differ from the reference program's by a relative error of at most 0.0003.
Values sent between devices are 32-bit elements; how exact they have to be, the bound alone decides.
A program may use at most 128 MiB of HBM per device.

```python
import math
import jax
import jax.numpy as jnp
from jax import lax

BLOCK = 128
REACH = 12
K = 4
ITERS = 3
NB = 768
POINTS = 98304
TARGETS = 32


def draw_pattern(key, part):
    blocks = jnp.arange(NB, dtype=jnp.int32)
    apart = jnp.concatenate([jnp.arange(-REACH, 0, dtype=jnp.int32), jnp.arange(1, REACH + 1, dtype=jnp.int32)])
    candidate = blocks[:, None] + apart[None, :]
    usable = (candidate >= 0) & (candidate < NB)
    raw = jax.random.randint(key, (TARGETS, NB, 2 * REACH), 0, 1 << 20, dtype=jnp.int32)
    order = jnp.arange(2 * REACH, dtype=jnp.int32)
    score = jnp.where(usable[None], raw * (2 * REACH) + order[None, None, :], -1)
    chosen_score, chosen_pos = lax.top_k(score, K - 1)
    chosen = jnp.take_along_axis(jnp.broadcast_to(candidate[None], score.shape), chosen_pos, axis=2)
    home = jnp.broadcast_to(blocks[None, :, None], (TARGETS, NB, 1))
    return jnp.concatenate([home, chosen], axis=2).astype(jnp.int32)


def surface_points(key, leading):
    first, second = jax.random.split(key)
    blocks = (jnp.arange(POINTS, dtype=jnp.int32) // BLOCK).astype(jnp.float32)
    spread = jax.random.uniform(first, leading + (1, POINTS), jnp.float32, 0.0, 1.0)
    along = (blocks + spread) / 32.0
    side = 0.25 + jnp.clip(0.12 * jax.random.normal(second, leading + (2, POINTS), jnp.float32), -0.25, 0.25)
    return jnp.concatenate([along, side], axis=len(leading)).astype(jnp.float32)


def draw_template_points(key, part):
    return surface_points(jax.random.fold_in(key, 11), ())


def draw_target_points(key, part):
    return surface_points(jax.random.fold_in(key, 23), (TARGETS,))


def shard_levels(rng, shape, cuts, least, top_value):
    loudness = 1.0
    for dim, blocks in cuts:
        draws = jax.random.uniform(jax.random.fold_in(jax.random.fold_in(rng, 6), dim), (blocks,), jnp.float32, least / len(cuts), top_value / len(cuts))
        loudness = loudness * jnp.repeat(jnp.exp(draws), shape[dim] // blocks).reshape((-1,) + (1,) * (len(shape) - 1 - dim))
    return loudness


def setup_inputs(seed: int = 0) -> dict:
    key_of = jax.random.split(jax.random.key(seed), 6)
    return {
        "template_points": draw_template_points(jax.random.fold_in(key_of[5], 71), 0),
        "template_mass": jnp.clip(jnp.exp(math.log(2.0) - 1.3862944 * jax.random.uniform(key_of[1], (POINTS,), jnp.float32) ** shard_levels(key_of[1], (POINTS,), ((0, 64),), -0.2, 0.2)), 0.5, 2.0),
        "target_points": draw_target_points(jax.random.fold_in(key_of[5], 71), 0),
        "target_mass": jnp.clip(jnp.exp(math.log(2.0) - 1.3862944 * jax.random.uniform(key_of[3], (TARGETS, POINTS), jnp.float32) ** shard_levels(key_of[3], (TARGETS, POINTS), ((0, 8), (1, 64)), -0.2, 0.2)), 0.5, 2.0),
        "pattern": draw_pattern(jax.random.fold_in(key_of[5], 71), 0),
    }


entropic = 0.02
marginal = 0.5
lowest = -1.0e30


def pair_costs(xb, coords):
    diff = xb[:, :, :, None, None] - coords[:, :, None, :, :]
    return 0.5 * jnp.sum(diff * diff, axis=1)


def template_update(cost, logb_pairs, g_pairs):
    shrink = marginal / (marginal + entropic)
    arg = logb_pairs[:, None] + (g_pairs[:, None] - cost) / entropic
    top = jnp.max(arg, axis=(2, 3))
    total = jnp.sum(jnp.exp(arg - top[:, :, None, None]), axis=(2, 3))
    return -shrink * entropic * (top + jnp.log(total))


def position_term(xb, coords, cost, log_a, logb_pairs, f_now, g_pairs):
    plan = jnp.exp(log_a[:, :, None, None] + logb_pairs[:, None] + (f_now[:, :, None, None] + g_pairs[:, None] - cost) / entropic)
    rows = jnp.sum(plan, axis=(2, 3))
    pulled = jnp.einsum('bikj,bckj->bci', plan, coords, precision=lax.Precision.HIGHEST)
    return xb * rows[:, None, :] - pulled


def reference(template_points, template_mass, target_points, target_mass, pattern):
    shrink = marginal / (marginal + entropic)
    xb = template_points.reshape(3, NB, BLOCK).transpose(1, 0, 2)
    log_a = jnp.log(template_mass).reshape(NB, BLOCK)

    def one_scan(members):
        points, mass, links = members
        yb = points.reshape(3, NB, BLOCK).transpose(1, 0, 2)
        log_b = jnp.log(mass).reshape(NB, BLOCK)
        coords = yb[links].transpose(0, 2, 1, 3)
        cost = pair_costs(xb, coords)
        logb_pairs = log_b[links]
        flat = links.reshape(-1)
        potential = jnp.zeros((NB, BLOCK), jnp.float32)
        f_now = jnp.zeros((NB, BLOCK), jnp.float32)
        for turn in range(ITERS):
            g_pairs = potential[links]
            f_now = template_update(cost, logb_pairs, g_pairs)
            arg = log_a[:, :, None, None] + (f_now[:, :, None, None] - cost) / entropic
            block_max = jnp.max(arg, axis=1)
            block_sum = jnp.sum(jnp.exp(arg - block_max[:, None]), axis=1)
            top = jnp.full((NB, BLOCK), lowest, jnp.float32).at[flat].max(block_max.reshape(-1, BLOCK))
            scaled = block_sum * jnp.exp(block_max - top[links])
            total = jnp.zeros((NB, BLOCK), jnp.float32).at[flat].add(scaled.reshape(-1, BLOCK))
            potential = -shrink * entropic * (top + jnp.log(total))
        g_pairs = potential[links]
        grad = position_term(xb, coords, cost, log_a, logb_pairs, f_now, g_pairs)
        return grad, potential

    grads, pots = lax.map(one_scan, (target_points, target_mass, pattern))
    position_grad = jnp.sum(grads, axis=0).transpose(1, 0, 2).reshape(3, POINTS)
    return position_grad, pots.reshape(TARGETS, POINTS)
```

```python
import functools
import math

import jax
import jax.numpy as jnp
from jax import lax
from jax.experimental import pallas as pl
from jax.experimental.pallas import tpu as pltpu
from jax.sharding import PartitionSpec as P

BLOCK = 128
REACH = 12
ITERS = 3

entropic = 0.02
marginal = 0.5
lowest = -1e30
shrink = marginal / (marginal + entropic)
unit = math.log2(math.e) / entropic

MESH = pl.DeviceIdType.MESH
ROWS = 16
SPAN = 3 * ROWS
OWN = slice(ROWS, 2 * ROWS)


def kernel(group, blk, pairs, count, peers, refs, outs, scratch):
    xp_ref, xm_ref, yp_ref, ym_ref, links_ref = refs
    grad_ref, pot_ref = outs
    s = scratch
    me = lax.axis_index("pts")
    mine = lax.axis_index("tgt")
    upper = lax.rem(me + 1, count)
    lower = lax.rem(me + count - 1, count)
    base = me * blk

    barrier = pltpu.get_barrier_semaphore()
    for side in (lower, upper):
        pl.semaphore_signal(barrier, inc=1, device_id={"pts": side}, device_id_type=MESH)
    for step in range(1, peers):
        pl.semaphore_signal(
            barrier, inc=1, device_id={"tgt": lax.rem(mine + step, peers)}, device_id_type=MESH
        )

    def both_ways(src_lower, src_upper, dst_lower, dst_upper, send, recv):
        down = pltpu.make_async_remote_copy(
            src_ref=src_lower, dst_ref=dst_upper, send_sem=send.at[0], recv_sem=recv.at[1],
            device_id={"pts": lower}, device_id_type=MESH,
        )
        up = pltpu.make_async_remote_copy(
            src_ref=src_upper, dst_ref=dst_lower, send_sem=send.at[1], recv_sem=recv.at[0],
            device_id={"pts": upper}, device_id_type=MESH,
        )
        return down, up

    def coord_copies(t):
        win = s["coord"][t]
        own = win.at[:, pl.ds(ROWS, ROWS)]
        return both_ways(
            own, own, win.at[:, pl.ds(0, ROWS)], win.at[:, pl.ds(2 * ROWS, ROWS)],
            s["c_send"].at[t], s["c_recv"].at[t],
        )

    def dual_copies(t):
        win = s["dual"][t]
        own = win.at[pl.ds(ROWS, ROWS)]
        return both_ways(
            own, own, win.at[pl.ds(0, ROWS)], win.at[pl.ds(2 * ROWS, ROWS)],
            s["d_send"].at[t], s["d_recv"].at[t],
        )

    def part_copies(t):
        win = s["part"].at[t]
        return both_ways(
            win.at[pl.ds(0, ROWS)], win.at[pl.ds(2 * ROWS, ROWS)],
            s["got"].at[t, 0], s["got"].at[t, 1],
            s["p_send"].at[t], s["p_recv"].at[t],
        )

    def start(copies):
        for c in copies:
            c.start()

    def wait_send(copies):
        for c in copies:
            c.wait_send()

    def wait_recv(copies):
        for c in copies:
            c.wait_recv()

    for t in range(group):
        for c in range(3):
            s["coord"][t][c, OWN] = jnp.zeros((ROWS, BLOCK), jnp.float32)
            for q in range(blk):
                s["coord"][t][c, ROWS + q : ROWS + q + 1] = yp_ref[t, c : c + 1, q * BLOCK : (q + 1) * BLOCK]
        s["logb"][t] = jnp.zeros((ROWS, BLOCK), jnp.float32)
        for q in range(blk):
            s["logb"][t, q : q + 1] = jnp.log2(ym_ref[t : t + 1, q * BLOCK : (q + 1) * BLOCK])
        s["dual"][t][OWN] = s["logb"][t]

    pl.semaphore_wait(barrier, 2 + peers - 1)
    for t in range(group):
        start(coord_copies(t))
        start(dual_copies(t))

    def columns(p, _):
        lanes = pl.ds(pl.multiple_of(p * BLOCK, BLOCK), BLOCK)
        for c in range(3):
            row = xp_ref[c : c + 1, lanes]
            s["xcol"][c, p] = jnp.transpose(jnp.broadcast_to(row, (BLOCK, BLOCK)))
        row = jnp.log2(xm_ref[:, lanes])
        s["acol"][p] = jnp.transpose(jnp.broadcast_to(row, (BLOCK, BLOCK)))
        return 0

    lax.fori_loop(0, blk, columns, 0)

    rows_iota = lax.broadcasted_iota(jnp.int32, (SPAN, BLOCK), 0)

    def window_row(t, p, k):
        w = jnp.clip(links_ref[t, p, k] - base + REACH, 0, blk + 2 * REACH - 1)
        pad = ROWS - blk
        return w + jnp.where(w >= blk, pad, 0) + jnp.where(w >= 2 * blk, pad, 0)

    def sweep(t, first, last):
        cost = s["cost"]

        def body(p, _):
            where = [ROWS + p] + [window_row(t, p, k) for k in range(1, pairs)]
            duals = [s["dual"][t][pl.ds(w, 1), :] for w in where]
            if first:
                for k in range(pairs):
                    y = [s["coord"][t][c, pl.ds(where[k], 1), :] for c in range(3)]
                    for r in range(0, BLOCK, 32):
                        d = [s["xcol"][c, p, r : r + 32] - y[c] for c in range(3)]
                        total = d[0] * d[0] + d[1] * d[1] + d[2] * d[2]
                        cost[t, p, k, r : r + 32] = total * (0.5 * unit)
            heads = []
            for r in range(0, BLOCK, 32):
                args = [duals[k] - cost[t, p, k, r : r + 32] for k in range(pairs)]
                top = functools.reduce(jnp.maximum, args)
                top = jnp.max(top, axis=1, keepdims=True)
                total = functools.reduce(jnp.add, [jnp.exp2(a - top) for a in args])
                total = jnp.sum(total, axis=1, keepdims=True)
                f = (top + jnp.log2(total)) * (-shrink)
                heads.append(s["acol"][p, r : r + 32] + f)
            head = jnp.concatenate(heads, axis=0)
            terms = []
            for k in range(pairs):
                arg = head - cost[t, p, k]
                top = jnp.max(arg, axis=0, keepdims=True)
                h = jnp.exp2(arg - top)
                if last:
                    cost[t, p, k] = h
                    s["tops"][t, p, k : k + 1] = top
                terms.append(top + jnp.log2(jnp.sum(h, axis=0, keepdims=True)))
            picked = jnp.where(rows_iota == where[0], terms[0], lowest)
            for k in range(1, pairs):
                picked = jnp.where(rows_iota == where[k], terms[k], picked)
            s["picked"][p] = picked
            s["best"][...] = jnp.maximum(s["best"][...], picked)
            return 0

        s["best"][...] = jnp.full((SPAN, BLOCK), lowest, jnp.float32)
        lax.fori_loop(0, blk, body, 0)
        best = s["best"][...]

        def add(p, total):
            return total + jnp.exp2(s["picked"][p] - best)

        total = lax.fori_loop(0, blk, add, jnp.zeros((SPAN, BLOCK), jnp.float32), unroll=True)
        if not first:
            wait_send(part_copies(t))
        s["part"][t] = best + jnp.log2(total)
        start(part_copies(t))

    def settle(t):
        wait_recv(part_copies(t))
        own = s["part"][t, OWN]
        sides = [s["got"][t, 0], s["got"][t, 1]]
        top = jnp.maximum(jnp.maximum(own, sides[0]), sides[1])
        total = jnp.exp2(own - top) + jnp.exp2(sides[0] - top) + jnp.exp2(sides[1] - top)
        g = (top + jnp.log2(total)) * (-shrink)
        wait_send(dual_copies(t))
        s["dual"][t][OWN] = s["logb"][t] + g
        start(dual_copies(t))
        return g

    def pull(t, first):
        acc = s["acc"]

        def body(p, _):
            where = [ROWS + p] + [window_row(t, p, k) for k in range(1, pairs)]
            scale, y = [], []
            for k in range(pairs):
                scale.append(jnp.exp2(s["tops"][t, p, k : k + 1] + s["dual"][t][pl.ds(where[k], 1), :]))
                y.append([s["coord"][t][c, pl.ds(where[k], 1), :] for c in range(3)])
            for r in range(0, BLOCK, 32):
                sums = [None] * 4 if first else [acc[p, c, r : r + 32] for c in range(4)]
                for k in range(pairs):
                    plan = s["cost"][t, p, k, r : r + 32] * scale[k]
                    new = [plan * y[k][c] for c in range(3)] + [plan]
                    sums = [b if a is None else a + b for a, b in zip(sums, new)]
                for c in range(4):
                    acc[p, c, r : r + 32] = sums[c]
            return 0

        lax.fori_loop(0, blk, body, 0)

    steps = [(turn, t) for turn in range(ITERS) for t in range(group)]
    for at, (turn, t) in enumerate(steps):
        if turn == 0:
            wait_recv(coord_copies(t))
        wait_recv(dual_copies(t))
        sweep(t, turn == 0, turn == ITERS - 1)
        if at:
            before, u = steps[at - 1]
            g = settle(u)
            if before == ITERS - 1:
                pot_ref[u] = g * (1.0 / unit)

    wait_recv(dual_copies(0))
    pull(0, True)
    pot_ref[group - 1] = settle(group - 1) * (1.0 / unit)
    for t in range(1, group):
        wait_recv(dual_copies(t))
        pull(t, False)

    s["grads"][mine] = jnp.zeros(s["grads"].shape[1:], jnp.float32)

    def finish(p, _):
        rows = s["acc"][p, 3]
        for c in range(3):
            part = s["xcol"][c, p] * rows - s["acc"][p, c]
            s["grads"][mine, pl.ds(c * ROWS + p, 1), :] = jnp.sum(jnp.transpose(part), axis=0, keepdims=True)
        return 0

    lax.fori_loop(0, blk, finish, 0)

    def grad_copy(to, slot):
        return pltpu.make_async_remote_copy(
            src_ref=s["grads"].at[mine], dst_ref=s["grads"].at[slot],
            send_sem=s["g_send"].at[to], recv_sem=s["g_recv"].at[slot],
            device_id={"tgt": to}, device_id_type=MESH,
        )

    others = [lax.rem(mine + step, peers) for step in range(1, peers)]
    for q in others:
        grad_copy(q, mine).start()
    for t in range(group):
        wait_send(coord_copies(t))
        wait_send(dual_copies(t))
        wait_send(part_copies(t))
    for q in others:
        grad_copy(q, q).wait_recv()
    total = s["grads"][0]
    for q in range(1, peers):
        total = total + s["grads"][q]
    for c in range(3):
        grad_ref[c] = total[c * ROWS : (c + 1) * ROWS]
    for q in others:
        grad_copy(q, mine).wait_send()


def shards(template_points, template_mass, target_points, target_mass, pattern):
    group, blk, pairs = pattern.shape
    width = blk * BLOCK
    count = lax.axis_size("pts")
    peers = lax.axis_size("tgt")
    f32 = jnp.float32

    names = {
        "coord": [pltpu.VMEM((3, SPAN, BLOCK), f32) for _ in range(group)],
        "dual": [pltpu.VMEM((SPAN, BLOCK), f32) for _ in range(group)],
        "logb": pltpu.VMEM((group, ROWS, BLOCK), f32),
        "part": pltpu.VMEM((group, SPAN, BLOCK), f32),
        "got": pltpu.VMEM((group, 2, ROWS, BLOCK), f32),
        "cost": pltpu.VMEM((group, blk, pairs, BLOCK, BLOCK), f32),
        "xcol": pltpu.VMEM((3, blk, BLOCK, BLOCK), f32),
        "acol": pltpu.VMEM((blk, BLOCK, BLOCK), f32),
        "tops": pltpu.VMEM((group, blk, 8, BLOCK), f32),
        "picked": pltpu.VMEM((blk, SPAN, BLOCK), f32),
        "best": pltpu.VMEM((SPAN, BLOCK), f32),
        "acc": pltpu.VMEM((blk, 4, BLOCK, BLOCK), f32),
        "grads": pltpu.VMEM((peers, SPAN, BLOCK), f32),
        "c_send": pltpu.SemaphoreType.DMA((group, 2)),
        "c_recv": pltpu.SemaphoreType.DMA((group, 2)),
        "d_send": pltpu.SemaphoreType.DMA((group, 2)),
        "d_recv": pltpu.SemaphoreType.DMA((group, 2)),
        "p_send": pltpu.SemaphoreType.DMA((group, 2)),
        "p_recv": pltpu.SemaphoreType.DMA((group, 2)),
        "g_send": pltpu.SemaphoreType.DMA((peers,)),
        "g_recv": pltpu.SemaphoreType.DMA((peers,)),
    }
    flat, tree = jax.tree.flatten(names)

    def run(*refs):
        kernel(group, blk, pairs, count, peers, refs[:5], refs[5:7], jax.tree.unflatten(tree, refs[7:]))

    whole = pl.BlockSpec(memory_space=pltpu.VMEM)
    elements = group * blk * pairs * BLOCK * BLOCK
    grad, pots = pl.pallas_call(
        run,
        out_shape=(
            jax.ShapeDtypeStruct((3, ROWS, BLOCK), f32),
            jax.ShapeDtypeStruct((group, ROWS, BLOCK), f32),
        ),
        in_specs=[whole, whole, whole, whole, pl.BlockSpec(memory_space=pltpu.SMEM)],
        out_specs=(whole, whole),
        scratch_shapes=flat,
        compiler_params=pltpu.CompilerParams(
            collective_id=0, has_side_effects=True, vmem_limit_bytes=48 * 1024 * 1024
        ),
        cost_estimate=pl.CostEstimate(
            flops=40 * elements, bytes_accessed=200000, transcendentals=6 * elements
        ),
        name="sinkhorn",
    )(template_points, template_mass.reshape(1, width), target_points, target_mass, pattern)
    return grad[:, :blk].reshape(3, width), pots[:, :blk].reshape(group, width)


def solution(mesh):
    placed = (
        P(None, "pts"),
        P("pts"),
        P("tgt", None, "pts"),
        P("tgt", "pts"),
        P("tgt", "pts", None),
    )
    return jax.shard_map(
        shards,
        mesh=mesh,
        in_specs=placed,
        out_specs=(P(None, "pts"), P("tgt", "pts")),
        check_vma=False,
    )
```

```python
import functools
import math

import jax
import jax.numpy as jnp
from jax import lax
from jax.experimental import pallas as pl
from jax.experimental.pallas import tpu as pltpu
from jax.sharding import PartitionSpec as P

BLOCK = 128
REACH = 12
ITERS = 3

entropic = 0.02
marginal = 0.5
lowest = -1e30
shrink = marginal / (marginal + entropic)
unit = math.log2(math.e) / entropic

MESH = pl.DeviceIdType.MESH
ROWS = 16
SPAN = 3 * ROWS
OWN = slice(ROWS, 2 * ROWS)
CORES = 2


def kernel(group, blk, pairs, count, peers, refs, outs, scratch):
    xp_ref, xm_ref, yp_ref, ym_ref, links_ref = refs
    grad_ref, pot_ref = outs
    s = scratch
    me = lax.axis_index("pts")
    mine = lax.axis_index("tgt")
    chips = peers // CORES
    chip = mine // CORES
    base = me * blk

    def at_distance(step):
        return {"pts": lax.rem(me + count + step, count)}

    sibling = {"tgt": chip * CORES + 1 - lax.rem(mine, CORES)}

    def same_core(step):
        return {"tgt": lax.rem(mine + step * CORES, peers)}

    greeted = [at_distance(step) for step in (-2, -1, 1, 2)]
    greeted += [sibling] + [same_core(step) for step in range(1, chips)]
    barrier = pltpu.get_barrier_semaphore()
    for other in greeted:
        pl.semaphore_signal(barrier, inc=1, device_id=other, device_id_type=MESH)

    def remote(src, dst, send, recv, to):
        return pltpu.make_async_remote_copy(
            src_ref=src, dst_ref=dst, send_sem=send, recv_sem=recv, device_id=to, device_id_type=MESH
        )

    def coord_copies(t):
        win, send, recv = s["coord"][t], s["c_send"].at[t], s["c_recv"].at[t]
        own = win.at[:, pl.ds(ROWS, ROWS)]
        return [
            remote(own, win.at[:, pl.ds(2 * ROWS, ROWS)], send.at[0], recv.at[0], at_distance(-1)),
            remote(own, win.at[:, pl.ds(0, ROWS)], send.at[1], recv.at[1], at_distance(1)),
        ]

    def part_copies(turn, t):
        part, got = s["part"].at[turn, t], s["got"].at[turn, t]
        send, recv = s["p_send"].at[turn, t], s["p_recv"].at[turn, t]
        lower, upper = pl.ds(0, ROWS), pl.ds(2 * ROWS, ROWS)
        not_lower, not_upper = pl.ds(ROWS, 2 * ROWS), pl.ds(0, 2 * ROWS)
        return [
            remote(part.at[lower], got.at[0, upper], send.at[0], recv.at[0], at_distance(-2)),
            remote(part.at[upper], got.at[1, lower], send.at[1], recv.at[1], at_distance(2)),
            remote(part.at[not_upper], got.at[1, not_lower], send.at[2], recv.at[2], at_distance(-1)),
            remote(part.at[not_lower], got.at[0, not_upper], send.at[3], recv.at[3], at_distance(1)),
        ]

    def start(copies):
        for c in copies:
            c.start()

    def wait_send(copies):
        for c in copies:
            c.wait_send()

    def wait_recv(copies):
        for c in copies:
            c.wait_recv()

    for t in range(group):
        for q in range(blk):
            lanes = slice(q * BLOCK, (q + 1) * BLOCK)
            for c in range(3):
                s["coord"][t][c, ROWS + q : ROWS + q + 1] = yp_ref[c, t : t + 1, lanes]
            s["coord"][t][3, ROWS + q : ROWS + q + 1] = jnp.log2(ym_ref[t : t + 1, lanes])
        for c in range(4):
            s["coord"][t][c, ROWS + blk : 2 * ROWS] = jnp.zeros((ROWS - blk, BLOCK), jnp.float32)

    pl.semaphore_wait(barrier, len(greeted))
    for t in range(group):
        start(coord_copies(t))

    def columns(p, _):
        lanes = pl.ds(pl.multiple_of(p * BLOCK, BLOCK), BLOCK)
        for c in range(3):
            row = xp_ref[c : c + 1, lanes]
            s["xcol"][c, p] = jnp.transpose(jnp.broadcast_to(row, (BLOCK, BLOCK)))
        row = jnp.log2(xm_ref[:, lanes])
        s["acol"][p] = jnp.transpose(jnp.broadcast_to(row, (BLOCK, BLOCK)))
        return 0

    lax.fori_loop(0, blk, columns, 0, unroll=2)

    rows_iota = lax.broadcasted_iota(jnp.int32, (SPAN, BLOCK), 0)

    def window_row(t, p, k):
        if k == 0:
            return ROWS + p
        w = jnp.clip(links_ref[t, k, p] - base + REACH, 0, blk + 2 * REACH - 1)
        pad = ROWS - blk
        return w + jnp.where(w >= blk, pad, 0) + jnp.where(w >= 2 * blk, pad, 0)

    def sweep(turn, t):
        first, last = turn == 0, turn == ITERS - 1
        cost = s["cost"]

        def body(p, _):
            where = [window_row(t, p, k) for k in range(pairs)]
            if first:
                duals = [s["coord"][t][3, pl.ds(w, 1), :] for w in where]
                for k in range(pairs):
                    y = [s["coord"][t][c, pl.ds(where[k], 1), :] for c in range(3)]
                    for r in range(0, BLOCK, 32):
                        d = [s["xcol"][c, p, r : r + 32] - y[c] for c in range(3)]
                        total = d[0] * d[0] + d[1] * d[1] + d[2] * d[2]
                        cost[t, p, k, r : r + 32] = total * (0.5 * unit)
            else:
                duals = [s["dual"][t, pl.ds(w, 1), :] for w in where]
            heads = []
            for r in range(0, BLOCK, 32):
                args = [duals[k] - cost[t, p, k, r : r + 32] for k in range(pairs)]
                top = functools.reduce(jnp.maximum, args)
                top = jnp.max(top, axis=1, keepdims=True)
                total = functools.reduce(jnp.add, [jnp.exp2(a - top) for a in args])
                total = jnp.sum(total, axis=1, keepdims=True)
                f = (top + jnp.log2(total)) * (-shrink)
                heads.append(s["acol"][p, r : r + 32] + f)
            head = jnp.concatenate(heads, axis=0)
            terms = []
            for k in range(pairs):
                arg = head - cost[t, p, k]
                top = jnp.max(arg, axis=0, keepdims=True)
                h = jnp.exp2(arg - top)
                if last:
                    cost[t, p, k] = h
                    s["tops"][t, p, k : k + 1] = top
                terms.append(top + jnp.log2(jnp.sum(h, axis=0, keepdims=True)))
            picked = jnp.where(rows_iota == where[0], terms[0], lowest)
            for k in range(1, pairs):
                picked = jnp.where(rows_iota == where[k], terms[k], picked)
            s["picked"][p] = picked
            s["best"][...] = jnp.maximum(s["best"][...], picked)
            return 0

        s["best"][...] = jnp.full((SPAN, BLOCK), lowest, jnp.float32)
        lax.fori_loop(0, blk, body, 0, unroll=4)
        best = s["best"][...]

        def add(p, total):
            return total + jnp.exp2(s["picked"][p] - best)

        total = lax.fori_loop(0, blk, add, jnp.zeros((SPAN, BLOCK), jnp.float32), unroll=True)
        s["part"][turn, t] = best + jnp.log2(total)
        start(part_copies(turn, t))

    def settle(turn, t):
        wait_recv(part_copies(turn, t))
        terms = [s["part"][turn, t], s["got"][turn, t, 0], s["got"][turn, t, 1]]
        top = functools.reduce(jnp.maximum, terms)
        total = functools.reduce(jnp.add, [jnp.exp2(a - top) for a in terms])
        g = (top + jnp.log2(total)) * (-shrink)
        s["dual"][t] = s["coord"][t][3] + g
        if turn == ITERS - 1:
            own = g[OWN] * (1.0 / unit)
            for q in range(blk):
                pot_ref[t : t + 1, q * BLOCK : (q + 1) * BLOCK] = own[q : q + 1]

    def pull(t):
        first, last = t == 0, t == group - 1
        acc = s["acc"]

        def body(p, _):
            where = [window_row(t, p, k) for k in range(pairs)]
            scale, y = [], []
            for k in range(pairs):
                scale.append(jnp.exp2(s["tops"][t, p, k : k + 1] + s["dual"][t, pl.ds(where[k], 1), :]))
                y.append([s["coord"][t][c, pl.ds(where[k], 1), :] for c in range(3)])
            parts = []
            for r in range(0, BLOCK, 32):
                sums = [None] * 4 if first else [acc[p, c, r : r + 32] for c in range(4)]
                for k in range(pairs):
                    plan = s["cost"][t, p, k, r : r + 32] * scale[k]
                    new = [plan * y[k][c] for c in range(3)] + [plan]
                    sums = [b if a is None else a + b for a, b in zip(sums, new)]
                if last:
                    parts.append([s["xcol"][c, p, r : r + 32] * sums[3] - sums[c] for c in range(3)])
                else:
                    for c in range(4):
                        acc[p, c, r : r + 32] = sums[c]
            if last:
                for c in range(3):
                    whole = jnp.transpose(jnp.concatenate([a[c] for a in parts], axis=0))
                    s["grad"][pl.ds(c * ROWS + p, 1), :] = jnp.sum(whole, axis=0, keepdims=True)
            return 0

        lax.fori_loop(0, blk, body, 0, unroll=2)

    for turn in range(ITERS):
        for t in range(group):
            if turn == 0:
                wait_recv(coord_copies(t))
            else:
                settle(turn - 1, t)
            sweep(turn, t)

    s["grad"][...] = jnp.zeros(s["grad"].shape, jnp.float32)
    for t in range(group):
        settle(ITERS - 1, t)
        pull(t)

    near = remote(s["grad"], s["grad_near"], s["n_send"], s["n_recv"], sibling)
    near.start()
    for t in range(group):
        wait_send(coord_copies(t))
        for turn in range(ITERS):
            wait_send(part_copies(turn, t))
    near.wait_recv()
    s["grad_far"][chip] = s["grad"][...] + s["grad_near"][...]

    def far(step, slot):
        return remote(
            s["grad_far"].at[chip], s["grad_far"].at[slot], s["f_send"].at[step - 1], s["f_recv"].at[slot],
            same_core(step),
        )

    for step in range(1, chips):
        far(step, chip).start()
    for step in range(1, chips):
        far(step, lax.rem(chip + step, chips)).wait_recv()
    total = s["grad_far"][0]
    for q in range(1, chips):
        total = total + s["grad_far"][q]
    for c in range(3):
        for q in range(blk):
            grad_ref[c : c + 1, q * BLOCK : (q + 1) * BLOCK] = total[c * ROWS + q : c * ROWS + q + 1]
    near.wait_send()
    for step in range(1, chips):
        far(step, chip).wait_send()


def shards(template_points, template_mass, target_points, target_mass, pattern):
    group, blk, pairs = pattern.shape
    width = blk * BLOCK
    count = lax.axis_size("pts")
    peers = lax.axis_size("tgt")
    f32 = jnp.float32

    names = {
        "coord": [pltpu.VMEM((4, SPAN, BLOCK), f32) for _ in range(group)],
        "dual": pltpu.VMEM((group, SPAN, BLOCK), f32),
        "part": pltpu.VMEM((ITERS, group, SPAN, BLOCK), f32),
        "got": pltpu.VMEM((ITERS, group, 2, SPAN, BLOCK), f32),
        "cost": pltpu.VMEM((group, blk, pairs, BLOCK, BLOCK), f32),
        "xcol": pltpu.VMEM((3, blk, BLOCK, BLOCK), f32),
        "acol": pltpu.VMEM((blk, BLOCK, BLOCK), f32),
        "tops": pltpu.VMEM((group, blk, 8, BLOCK), f32),
        "picked": pltpu.VMEM((blk, SPAN, BLOCK), f32),
        "best": pltpu.VMEM((SPAN, BLOCK), f32),
        "acc": pltpu.VMEM((blk, 4, BLOCK, BLOCK), f32),
        "grad": pltpu.VMEM((SPAN, BLOCK), f32),
        "grad_near": pltpu.VMEM((SPAN, BLOCK), f32),
        "grad_far": pltpu.VMEM((peers // CORES, SPAN, BLOCK), f32),
        "c_send": pltpu.SemaphoreType.DMA((group, 2)),
        "c_recv": pltpu.SemaphoreType.DMA((group, 2)),
        "p_send": pltpu.SemaphoreType.DMA((ITERS, group, 4)),
        "p_recv": pltpu.SemaphoreType.DMA((ITERS, group, 4)),
        "n_send": pltpu.SemaphoreType.DMA,
        "n_recv": pltpu.SemaphoreType.DMA,
        "f_send": pltpu.SemaphoreType.DMA((peers // CORES,)),
        "f_recv": pltpu.SemaphoreType.DMA((peers // CORES,)),
    }
    flat, tree = jax.tree.flatten(names)

    def run(*refs):
        kernel(group, blk, pairs, count, peers, refs[:5], refs[5:7], jax.tree.unflatten(tree, refs[7:]))

    whole = pl.BlockSpec(memory_space=pltpu.VMEM)
    elements = group * blk * pairs * BLOCK * BLOCK
    grad, pots = pl.pallas_call(
        run,
        out_shape=(
            jax.ShapeDtypeStruct((3, width), f32),
            jax.ShapeDtypeStruct((group, width), f32),
        ),
        in_specs=[whole, whole, whole, whole, pl.BlockSpec(memory_space=pltpu.SMEM)],
        out_specs=(whole, whole),
        scratch_shapes=flat,
        compiler_params=pltpu.CompilerParams(
            collective_id=0, has_side_effects=True, vmem_limit_bytes=48 * 1024 * 1024
        ),
        cost_estimate=pl.CostEstimate(
            flops=40 * elements, bytes_accessed=200000, transcendentals=6 * elements
        ),
        name="sinkhorn",
    )(
        template_points,
        template_mass.reshape(1, width),
        target_points.transpose(1, 0, 2),
        target_mass,
        pattern.transpose(0, 2, 1),
    )
    return grad, pots


def solution(mesh):
    placed = (
        P(None, "pts"),
        P("pts"),
        P("tgt", None, "pts"),
        P("tgt", "pts"),
        P("tgt", "pts", None),
    )
    return jax.shard_map(
        shards,
        mesh=mesh,
        in_specs=placed,
        out_specs=(P(None, "pts"), P("tgt", "pts")),
        check_vma=False,
    )
```

```python
import functools
import math

import jax
import jax.numpy as jnp
from jax import lax
from jax.experimental import pallas as pl
from jax.experimental.pallas import tpu as pltpu
from jax.sharding import PartitionSpec as P

BLOCK = 128
REACH = 12
ITERS = 3

entropic = 0.02
marginal = 0.5
lowest = -1e30
shrink = marginal / (marginal + entropic)
unit = math.log2(math.e) / entropic

MESH = pl.DeviceIdType.MESH
ROWS = 16
SPAN = 3 * ROWS
OWN = slice(ROWS, 2 * ROWS)
CORES = 2


def kernel(group, blk, pairs, count, peers, refs, outs, scratch):
    grad_ref, pot_ref = outs
    s = scratch
    held = ["yp", "ym", "xp", "xm", "links"]
    order = [2, 3, 0, 1, 4]
    loads = [
        pltpu.make_async_copy(refs[order[i]], s[name], s["l_sem"].at[i]) for i, name in enumerate(held)
    ]
    xp_ref, xm_ref, yp_ref, ym_ref, links_ref = (s[name] for name in ("xp", "xm", "yp", "ym", "links"))
    me = lax.axis_index("pts")
    mine = lax.axis_index("tgt")
    chips = peers // CORES
    chip = mine // CORES
    base = me * blk

    def at_distance(step):
        return {"pts": lax.rem(me + count + step, count)}

    sibling = {"tgt": chip * CORES + 1 - lax.rem(mine, CORES)}

    def same_core(step):
        return {"tgt": lax.rem(mine + step * CORES, peers)}

    greeted = [at_distance(step) for step in (-2, -1, 1, 2)]
    greeted += [sibling] + [same_core(step) for step in range(1, chips)]
    barrier = pltpu.get_barrier_semaphore()
    for other in greeted:
        pl.semaphore_signal(barrier, inc=1, device_id=other, device_id_type=MESH)

    def remote(src, dst, send, recv, to):
        return pltpu.make_async_remote_copy(
            src_ref=src, dst_ref=dst, send_sem=send, recv_sem=recv, device_id=to, device_id_type=MESH
        )

    def coord_copies(t):
        win, send, recv = s["coord"][t], s["c_send"].at[t], s["c_recv"].at[t]
        own = win.at[:, pl.ds(ROWS, ROWS)]
        return [
            remote(own, win.at[:, pl.ds(2 * ROWS, ROWS)], send.at[0], recv.at[0], at_distance(-1)),
            remote(own, win.at[:, pl.ds(0, ROWS)], send.at[1], recv.at[1], at_distance(1)),
        ]

    def part_copies(turn, t):
        part, got = s["part"].at[turn, t], s["got"].at[turn, t]
        send, recv = s["p_send"].at[turn, t], s["p_recv"].at[turn, t]
        lower, upper = pl.ds(0, ROWS), pl.ds(2 * ROWS, ROWS)
        not_lower, not_upper = pl.ds(ROWS, 2 * ROWS), pl.ds(0, 2 * ROWS)
        return [
            remote(part.at[lower], got.at[0, upper], send.at[0], recv.at[0], at_distance(-2)),
            remote(part.at[upper], got.at[1, lower], send.at[1], recv.at[1], at_distance(2)),
            remote(part.at[not_upper], got.at[1, not_lower], send.at[2], recv.at[2], at_distance(-1)),
            remote(part.at[not_lower], got.at[0, not_upper], send.at[3], recv.at[3], at_distance(1)),
        ]

    def start(copies):
        for c in copies:
            c.start()

    def wait_send(copies):
        for c in copies:
            c.wait_send()

    def wait_recv(copies):
        for c in copies:
            c.wait_recv()

    for load in loads:
        load.start()
    loads[0].wait()
    loads[1].wait()
    for t in range(group):
        for q in range(blk):
            lanes = slice(q * BLOCK, (q + 1) * BLOCK)
            for c in range(3):
                row = yp_ref[c, t : t + 1, lanes]
                s["coord"][t][c, ROWS + q : ROWS + q + 1] = row
                s["own"][t, c, q : q + 1] = row
            s["coord"][t][3, ROWS + q : ROWS + q + 1] = jnp.log2(ym_ref[t : t + 1, lanes])
        for c in range(4):
            s["coord"][t][c, ROWS + blk : 2 * ROWS] = jnp.zeros((ROWS - blk, BLOCK), jnp.float32)

    pl.semaphore_wait(barrier, len(greeted))
    for t in range(group):
        start(coord_copies(t))

    for load in loads[2:]:
        load.wait()

    def columns(p, _):
        lanes = pl.ds(pl.multiple_of(p * BLOCK, BLOCK), BLOCK)
        for c in range(3):
            row = xp_ref[c : c + 1, lanes]
            s["xcol"][c, p] = jnp.transpose(jnp.broadcast_to(row, (BLOCK, BLOCK)))
        row = jnp.log2(xm_ref[lanes]).reshape(1, BLOCK)
        s["acol"][p] = jnp.transpose(jnp.broadcast_to(row, (BLOCK, BLOCK)))
        return 0

    lax.fori_loop(0, blk, columns, 0, unroll=2)

    def tile_cost(t, p, k, w):
        y = [s["coord"][t][c, pl.ds(w, 1), :] for c in range(3)]
        for r in range(0, BLOCK, 32):
            d = [s["xcol"][c, p, r : r + 32] - y[c] for c in range(3)]
            total = d[0] * d[0] + d[1] * d[1] + d[2] * d[2]
            s["cost"][t, p, k, r : r + 32] = total * (0.5 * unit)

    def own_tiles(p, _):
        for t in range(group):
            for r in range(0, BLOCK, 32):
                y = [s["own"][t, c, pl.ds(p, 1), :] for c in range(3)]
                d = [s["xcol"][c, p, r : r + 32] - y[c] for c in range(3)]
                total = d[0] * d[0] + d[1] * d[1] + d[2] * d[2]
                s["cost"][t, p, 0, r : r + 32] = total * (0.5 * unit)
        return 0

    lax.fori_loop(0, blk, own_tiles, 0)

    rows_iota = lax.broadcasted_iota(jnp.int32, (SPAN, BLOCK), 0)

    def window_row(t, p, k):
        if k == 0:
            return ROWS + p
        w = jnp.clip(links_ref[t, k, p] - base + REACH, 0, blk + 2 * REACH - 1)
        pad = ROWS - blk
        return w + jnp.where(w >= blk, pad, 0) + jnp.where(w >= 2 * blk, pad, 0)

    def sweep(turn, t):
        first, last = turn == 0, turn == ITERS - 1
        cost = s["cost"]

        def body(p, _):
            where = [window_row(t, p, k) for k in range(pairs)]
            if first:
                duals = [s["coord"][t][3, pl.ds(w, 1), :] for w in where]
                for k in range(1, pairs):
                    tile_cost(t, p, k, where[k])
            else:
                duals = [s["dual"][t, pl.ds(w, 1), :] for w in where]
            heads = []
            for r in range(0, BLOCK, 32):
                costs = [cost[t, p, k, r : r + 32] for k in range(pairs)]
                args = [duals[k] - costs[k] for k in range(pairs)]
                if first:
                    top = -jnp.min(functools.reduce(jnp.minimum, costs), axis=1, keepdims=True)
                else:
                    top = jnp.max(functools.reduce(jnp.maximum, args), axis=1, keepdims=True)
                total = functools.reduce(jnp.add, [jnp.exp2(a - top) for a in args])
                total = jnp.sum(total, axis=1, keepdims=True)
                f = (top + jnp.log2(total)) * (-shrink)
                heads.append(s["acol"][p, r : r + 32] + f)
            head = jnp.concatenate(heads, axis=0)
            terms = []
            for k in range(pairs):
                arg = head - cost[t, p, k]
                top = jnp.max(arg, axis=0, keepdims=True)
                h = jnp.exp2(arg - top)
                if last:
                    cost[t, p, k] = h
                    s["tops"][t, p, k : k + 1] = top
                terms.append(top + jnp.log2(jnp.sum(h, axis=0, keepdims=True)))
            picked = jnp.where(rows_iota == where[0], terms[0], lowest)
            for k in range(1, pairs):
                picked = jnp.where(rows_iota == where[k], terms[k], picked)
            s["picked"][p] = picked
            s["best"][...] = jnp.maximum(s["best"][...], picked)
            return 0

        s["best"][...] = jnp.full((SPAN, BLOCK), lowest, jnp.float32)
        lax.fori_loop(0, blk, body, 0, unroll=4)
        best = s["best"][...]

        def add(p, total):
            return total + jnp.exp2(s["picked"][p] - best)

        total = lax.fori_loop(0, blk, add, jnp.zeros((SPAN, BLOCK), jnp.float32), unroll=True)
        s["part"][turn, t] = best + jnp.log2(total)
        start(part_copies(turn, t))

    def settle(turn, t):
        wait_recv(part_copies(turn, t))
        terms = [s["part"][turn, t], s["got"][turn, t, 0], s["got"][turn, t, 1]]
        top = functools.reduce(jnp.maximum, terms)
        total = functools.reduce(jnp.add, [jnp.exp2(a - top) for a in terms])
        g = (top + jnp.log2(total)) * (-shrink)
        s["dual"][t] = s["coord"][t][3] + g
        if turn == ITERS - 1:
            own = g[OWN] * (1.0 / unit)
            for q in range(blk):
                pot_ref[t : t + 1, q * BLOCK : (q + 1) * BLOCK] = own[q : q + 1]

    def pull(t):
        first, last = t == 0, t == group - 1
        acc = s["acc"]

        def body(p, _):
            where = [window_row(t, p, k) for k in range(pairs)]
            scale, y = [], []
            for k in range(pairs):
                scale.append(jnp.exp2(s["tops"][t, p, k : k + 1] + s["dual"][t, pl.ds(where[k], 1), :]))
                y.append([s["coord"][t][c, pl.ds(where[k], 1), :] for c in range(3)])
            parts = []
            for r in range(0, BLOCK, 32):
                sums = [None] * 4 if first else [acc[p, c, r : r + 32] for c in range(4)]
                for k in range(pairs):
                    plan = s["cost"][t, p, k, r : r + 32] * scale[k]
                    new = [plan * y[k][c] for c in range(3)] + [plan]
                    sums = [b if a is None else a + b for a, b in zip(sums, new)]
                if last:
                    parts.append([s["xcol"][c, p, r : r + 32] * sums[3] - sums[c] for c in range(3)])
                else:
                    for c in range(4):
                        acc[p, c, r : r + 32] = sums[c]
            if last:
                for c in range(3):
                    whole = jnp.transpose(jnp.concatenate([a[c] for a in parts], axis=0))
                    s["grad"][pl.ds(c * ROWS + p, 1), :] = jnp.sum(whole, axis=0, keepdims=True)
            return 0

        lax.fori_loop(0, blk, body, 0, unroll=2)

    for turn in range(ITERS):
        for t in range(group):
            if turn == 0:
                wait_recv(coord_copies(t))
            else:
                settle(turn - 1, t)
            sweep(turn, t)

    s["grad"][...] = jnp.zeros(s["grad"].shape, jnp.float32)
    for t in range(group):
        settle(ITERS - 1, t)
        pull(t)

    near = remote(s["grad"], s["grad_near"], s["n_send"], s["n_recv"], sibling)
    near.start()
    for t in range(group):
        wait_send(coord_copies(t))
        for turn in range(ITERS):
            wait_send(part_copies(turn, t))
    near.wait_recv()
    s["grad_far"][chip] = s["grad"][...] + s["grad_near"][...]

    def far(step, slot):
        return remote(
            s["grad_far"].at[chip], s["grad_far"].at[slot], s["f_send"].at[step - 1], s["f_recv"].at[slot],
            same_core(step),
        )

    for step in range(1, chips):
        far(step, chip).start()
    for step in range(1, chips):
        far(step, lax.rem(chip + step, chips)).wait_recv()
    total = s["grad_far"][0]
    for q in range(1, chips):
        total = total + s["grad_far"][q]
    for c in range(3):
        for q in range(blk):
            grad_ref[c : c + 1, q * BLOCK : (q + 1) * BLOCK] = total[c * ROWS + q : c * ROWS + q + 1]
    near.wait_send()
    for step in range(1, chips):
        far(step, chip).wait_send()


def shards(template_points, template_mass, target_points, target_mass, pattern):
    group, blk, pairs = pattern.shape
    width = blk * BLOCK
    count = lax.axis_size("pts")
    peers = lax.axis_size("tgt")
    f32 = jnp.float32

    names = {
        "xp": pltpu.VMEM((3, width), f32),
        "xm": pltpu.VMEM((width,), f32),
        "yp": pltpu.VMEM((3, group, width), f32),
        "ym": pltpu.VMEM((group, width), f32),
        "links": pltpu.SMEM((group, pairs, blk), jnp.int32),
        "l_sem": pltpu.SemaphoreType.DMA((5,)),
        "own": pltpu.VMEM((group, 3, ROWS, BLOCK), f32),
        "coord": [pltpu.VMEM((4, SPAN, BLOCK), f32) for _ in range(group)],
        "dual": pltpu.VMEM((group, SPAN, BLOCK), f32),
        "part": pltpu.VMEM((ITERS, group, SPAN, BLOCK), f32),
        "got": pltpu.VMEM((ITERS, group, 2, SPAN, BLOCK), f32),
        "cost": pltpu.VMEM((group, blk, pairs, BLOCK, BLOCK), f32),
        "xcol": pltpu.VMEM((3, blk, BLOCK, BLOCK), f32),
        "acol": pltpu.VMEM((blk, BLOCK, BLOCK), f32),
        "tops": pltpu.VMEM((group, blk, 8, BLOCK), f32),
        "picked": pltpu.VMEM((blk, SPAN, BLOCK), f32),
        "best": pltpu.VMEM((SPAN, BLOCK), f32),
        "acc": pltpu.VMEM((blk, 4, BLOCK, BLOCK), f32),
        "grad": pltpu.VMEM((SPAN, BLOCK), f32),
        "grad_near": pltpu.VMEM((SPAN, BLOCK), f32),
        "grad_far": pltpu.VMEM((peers // CORES, SPAN, BLOCK), f32),
        "c_send": pltpu.SemaphoreType.DMA((group, 2)),
        "c_recv": pltpu.SemaphoreType.DMA((group, 2)),
        "p_send": pltpu.SemaphoreType.DMA((ITERS, group, 4)),
        "p_recv": pltpu.SemaphoreType.DMA((ITERS, group, 4)),
        "n_send": pltpu.SemaphoreType.DMA,
        "n_recv": pltpu.SemaphoreType.DMA,
        "f_send": pltpu.SemaphoreType.DMA((peers // CORES,)),
        "f_recv": pltpu.SemaphoreType.DMA((peers // CORES,)),
    }
    flat, tree = jax.tree.flatten(names)

    def run(*refs):
        kernel(group, blk, pairs, count, peers, refs[:5], refs[5:7], jax.tree.unflatten(tree, refs[7:]))

    whole = pl.BlockSpec(memory_space=pltpu.VMEM)
    held = pl.BlockSpec(memory_space=pltpu.HBM)
    elements = group * blk * pairs * BLOCK * BLOCK
    grad, pots = pl.pallas_call(
        run,
        out_shape=(
            jax.ShapeDtypeStruct((3, width), f32),
            jax.ShapeDtypeStruct((group, width), f32),
        ),
        in_specs=[held] * 5,
        out_specs=(whole, whole),
        scratch_shapes=flat,
        compiler_params=pltpu.CompilerParams(
            collective_id=0, has_side_effects=True, vmem_limit_bytes=63 * 1024 * 1024
        ),
        cost_estimate=pl.CostEstimate(
            flops=40 * elements, bytes_accessed=200000, transcendentals=6 * elements
        ),
        name="sinkhorn",
    )(
        template_points,
        template_mass,
        target_points.transpose(1, 0, 2),
        target_mass,
        pattern.transpose(0, 2, 1),
    )
    return grad, pots


def solution(mesh):
    placed = (
        P(None, "pts"),
        P("pts"),
        P("tgt", None, "pts"),
        P("tgt", "pts"),
        P("tgt", "pts", None),
    )
    return jax.shard_map(
        shards,
        mesh=mesh,
        in_specs=placed,
        out_specs=(P(None, "pts"), P("tgt", "pts")),
        check_vma=False,
    )
```

```python
import functools
import math

import jax
import jax.numpy as jnp
from jax import lax
from jax.experimental import pallas as pl
from jax.experimental.pallas import tpu as pltpu
from jax.sharding import PartitionSpec as P

BLOCK = 128
REACH = 12
ITERS = 3

entropic = 0.02
marginal = 0.5
lowest = -1e30
shrink = marginal / (marginal + entropic)
unit = math.log2(math.e) / entropic

MESH = pl.DeviceIdType.MESH
ROWS = 16
SPAN = 3 * ROWS
OWN = slice(ROWS, 2 * ROWS)
CORES = 2


def kernel(group, blk, pairs, count, peers, refs, outs, scratch):
    grad_ref, pot_ref = outs
    s = scratch
    held = ["yp", "ym", "xp", "xm", "links"]
    order = [2, 3, 0, 1, 4]
    loads = [
        pltpu.make_async_copy(refs[order[i]], s[name], s["l_sem"].at[i]) for i, name in enumerate(held)
    ]
    xp_ref, xm_ref, yp_ref, ym_ref, links_ref = (s[name] for name in ("xp", "xm", "yp", "ym", "links"))
    me = lax.axis_index("pts")
    mine = lax.axis_index("tgt")
    chips = peers // CORES
    chip = mine // CORES
    base = me * blk

    def at_distance(step):
        return {"pts": lax.rem(me + count + step, count)}

    sibling = {"tgt": chip * CORES + 1 - lax.rem(mine, CORES)}

    def same_core(step):
        return {"tgt": lax.rem(mine + step * CORES, peers)}

    greeted = [at_distance(step) for step in (-2, -1, 1, 2)]
    greeted += [sibling] + [same_core(step) for step in range(1, chips)]
    barrier = pltpu.get_barrier_semaphore()
    for other in greeted:
        pl.semaphore_signal(barrier, inc=1, device_id=other, device_id_type=MESH)

    def remote(src, dst, send, recv, to):
        return pltpu.make_async_remote_copy(
            src_ref=src, dst_ref=dst, send_sem=send, recv_sem=recv, device_id=to, device_id_type=MESH
        )

    def coord_copies(t):
        win, send, recv = s["coord"][t], s["c_send"].at[t], s["c_recv"].at[t]
        own = win.at[:, pl.ds(ROWS, ROWS)]
        return [
            remote(own, win.at[:, pl.ds(2 * ROWS, ROWS)], send.at[0], recv.at[0], at_distance(-1)),
            remote(own, win.at[:, pl.ds(0, ROWS)], send.at[1], recv.at[1], at_distance(1)),
        ]

    def part_copies(turn, t):
        part, got = s["part"].at[turn, t], s["got"].at[turn, t]
        send, recv = s["p_send"].at[turn, t], s["p_recv"].at[turn, t]
        lower, upper = pl.ds(0, ROWS), pl.ds(2 * ROWS, ROWS)
        not_lower, not_upper = pl.ds(ROWS, 2 * ROWS), pl.ds(0, 2 * ROWS)
        return [
            remote(part.at[lower], got.at[0, upper], send.at[0], recv.at[0], at_distance(-2)),
            remote(part.at[upper], got.at[1, lower], send.at[1], recv.at[1], at_distance(2)),
            remote(part.at[not_upper], got.at[1, not_lower], send.at[2], recv.at[2], at_distance(-1)),
            remote(part.at[not_lower], got.at[0, not_upper], send.at[3], recv.at[3], at_distance(1)),
        ]

    def start(copies):
        for c in copies:
            c.start()

    def wait_send(copies):
        for c in copies:
            c.wait_send()

    def wait_recv(copies):
        for c in copies:
            c.wait_recv()

    for load in loads:
        load.start()
    loads[0].wait()
    loads[1].wait()
    for t in range(group):
        for q in range(blk):
            lanes = slice(q * BLOCK, (q + 1) * BLOCK)
            for c in range(3):
                row = yp_ref[c, t : t + 1, lanes]
                s["coord"][t][c, ROWS + q : ROWS + q + 1] = row
                s["own"][t, c, q : q + 1] = row
            s["coord"][t][3, ROWS + q : ROWS + q + 1] = jnp.log2(ym_ref[t : t + 1, lanes])
        for c in range(4):
            s["coord"][t][c, ROWS + blk : 2 * ROWS] = jnp.zeros((ROWS - blk, BLOCK), jnp.float32)

    pl.semaphore_wait(barrier, len(greeted))
    start(coord_copies(0))

    for load in loads[2:]:
        load.wait()

    def columns(p, _):
        lanes = pl.ds(pl.multiple_of(p * BLOCK, BLOCK), BLOCK)
        for c in range(3):
            row = xp_ref[c : c + 1, lanes]
            s["xcol"][c, p] = jnp.transpose(jnp.broadcast_to(row, (BLOCK, BLOCK)))
        row = jnp.log2(xm_ref[lanes]).reshape(1, BLOCK)
        s["acol"][p] = jnp.transpose(jnp.broadcast_to(row, (BLOCK, BLOCK)))
        return 0

    lax.fori_loop(0, blk, columns, 0, unroll=2)
    if group > 1:
        start(coord_copies(1))

    def tile_cost(t, p, k, w):
        y = [s["coord"][t][c, pl.ds(w, 1), :] for c in range(3)]
        for r in range(0, BLOCK, 32):
            d = [s["xcol"][c, p, r : r + 32] - y[c] for c in range(3)]
            total = d[0] * d[0] + d[1] * d[1] + d[2] * d[2]
            s["cost"][t, p, k, r : r + 32] = total * (0.5 * unit)

    def own_tiles(p, _):
        for t in range(group):
            for r in range(0, BLOCK, 32):
                y = [s["own"][t, c, pl.ds(p, 1), :] for c in range(3)]
                d = [s["xcol"][c, p, r : r + 32] - y[c] for c in range(3)]
                total = d[0] * d[0] + d[1] * d[1] + d[2] * d[2]
                s["cost"][t, p, 0, r : r + 32] = total * (0.5 * unit)
        return 0

    lax.fori_loop(0, blk, own_tiles, 0)
    for t in range(2, group):
        start(coord_copies(t))

    rows_iota = lax.broadcasted_iota(jnp.int32, (SPAN, BLOCK), 0)

    def window_row(t, p, k):
        if k == 0:
            return ROWS + p
        w = jnp.clip(links_ref[t, k, p] - base + REACH, 0, blk + 2 * REACH - 1)
        pad = ROWS - blk
        return w + jnp.where(w >= blk, pad, 0) + jnp.where(w >= 2 * blk, pad, 0)

    def sweep(turn, t):
        first, last = turn == 0, turn == ITERS - 1
        cost = s["cost"]

        def body(p, _):
            where = [window_row(t, p, k) for k in range(pairs)]
            if first:
                duals = [s["coord"][t][3, pl.ds(w, 1), :] for w in where]
                for k in range(1, pairs):
                    tile_cost(t, p, k, where[k])
            else:
                duals = [s["dual"][t, pl.ds(w, 1), :] for w in where]
            heads = []
            for r in range(0, BLOCK, 32):
                costs = [cost[t, p, k, r : r + 32] for k in range(pairs)]
                args = [duals[k] - costs[k] for k in range(pairs)]
                if first:
                    top = -jnp.min(functools.reduce(jnp.minimum, costs), axis=1, keepdims=True)
                else:
                    top = jnp.max(functools.reduce(jnp.maximum, args), axis=1, keepdims=True)
                total = functools.reduce(jnp.add, [jnp.exp2(a - top) for a in args])
                total = jnp.sum(total, axis=1, keepdims=True)
                f = (top + jnp.log2(total)) * (-shrink)
                heads.append(s["acol"][p, r : r + 32] + f)
            head = jnp.concatenate(heads, axis=0)
            terms = []
            for k in range(pairs):
                arg = head - cost[t, p, k]
                top = jnp.max(arg, axis=0, keepdims=True)
                h = jnp.exp2(arg - top)
                if last:
                    cost[t, p, k] = h
                    s["tops"][t, p, k : k + 1] = top
                terms.append(top + jnp.log2(jnp.sum(h, axis=0, keepdims=True)))
            picked = jnp.where(rows_iota == where[0], terms[0], lowest)
            for k in range(1, pairs):
                picked = jnp.where(rows_iota == where[k], terms[k], picked)
            s["picked"][p] = picked
            s["best"][...] = jnp.maximum(s["best"][...], picked)
            return 0

        s["best"][...] = jnp.full((SPAN, BLOCK), lowest, jnp.float32)
        lax.fori_loop(0, blk, body, 0, unroll=4)
        best = s["best"][...]

        def add(p, total):
            return total + jnp.exp2(s["picked"][p] - best)

        total = lax.fori_loop(0, blk, add, jnp.zeros((SPAN, BLOCK), jnp.float32), unroll=True)
        s["part"][turn, t] = best + jnp.log2(total)
        start(part_copies(turn, t))

    def settle(turn, t):
        wait_recv(part_copies(turn, t))
        terms = [s["part"][turn, t], s["got"][turn, t, 0], s["got"][turn, t, 1]]
        top = functools.reduce(jnp.maximum, terms)
        total = functools.reduce(jnp.add, [jnp.exp2(a - top) for a in terms])
        g = (top + jnp.log2(total)) * (-shrink)
        s["dual"][t] = s["coord"][t][3] + g
        if turn == ITERS - 1:
            own = g[OWN] * (1.0 / unit)
            for q in range(blk):
                pot_ref[t : t + 1, q * BLOCK : (q + 1) * BLOCK] = own[q : q + 1]

    def pull(t):
        first, last = t == 0, t == group - 1
        acc = s["acc"]

        def body(p, _):
            where = [window_row(t, p, k) for k in range(pairs)]
            scale, y = [], []
            for k in range(pairs):
                scale.append(jnp.exp2(s["tops"][t, p, k : k + 1] + s["dual"][t, pl.ds(where[k], 1), :]))
                y.append([s["coord"][t][c, pl.ds(where[k], 1), :] for c in range(3)])
            parts = []
            for r in range(0, BLOCK, 32):
                sums = [None] * 4 if first else [acc[p, c, r : r + 32] for c in range(4)]
                for k in range(pairs):
                    plan = s["cost"][t, p, k, r : r + 32] * scale[k]
                    new = [plan * y[k][c] for c in range(3)] + [plan]
                    sums = [b if a is None else a + b for a, b in zip(sums, new)]
                if last:
                    parts.append([s["xcol"][c, p, r : r + 32] * sums[3] - sums[c] for c in range(3)])
                else:
                    for c in range(4):
                        acc[p, c, r : r + 32] = sums[c]
            if last:
                for c in range(3):
                    whole = jnp.transpose(jnp.concatenate([a[c] for a in parts], axis=0))
                    s["grad"][pl.ds(c * ROWS + p, 1), :] = jnp.sum(whole, axis=0, keepdims=True)
            return 0

        lax.fori_loop(0, blk, body, 0, unroll=2)

    for turn in range(ITERS):
        for t in range(group):
            if turn == 0:
                wait_recv(coord_copies(t))
            else:
                settle(turn - 1, t)
            sweep(turn, t)

    s["grad"][...] = jnp.zeros(s["grad"].shape, jnp.float32)
    for t in range(group):
        settle(ITERS - 1, t)
        pull(t)

    near = remote(s["grad"], s["grad_near"], s["n_send"], s["n_recv"], sibling)
    near.start()
    for t in range(group):
        wait_send(coord_copies(t))
        for turn in range(ITERS):
            wait_send(part_copies(turn, t))
    near.wait_recv()
    s["grad_far"][chip] = s["grad"][...] + s["grad_near"][...]

    def far(step, slot):
        return remote(
            s["grad_far"].at[chip], s["grad_far"].at[slot], s["f_send"].at[step - 1], s["f_recv"].at[slot],
            same_core(step),
        )

    for step in range(1, chips):
        far(step, chip).start()
    for step in range(1, chips):
        far(step, lax.rem(chip + step, chips)).wait_recv()
    total = s["grad_far"][0]
    for q in range(1, chips):
        total = total + s["grad_far"][q]
    for c in range(3):
        for q in range(blk):
            grad_ref[c : c + 1, q * BLOCK : (q + 1) * BLOCK] = total[c * ROWS + q : c * ROWS + q + 1]
    near.wait_send()
    for step in range(1, chips):
        far(step, chip).wait_send()


def shards(template_points, template_mass, target_points, target_mass, pattern):
    group, blk, pairs = pattern.shape
    width = blk * BLOCK
    count = lax.axis_size("pts")
    peers = lax.axis_size("tgt")
    f32 = jnp.float32

    names = {
        "xp": pltpu.VMEM((3, width), f32),
        "xm": pltpu.VMEM((width,), f32),
        "yp": pltpu.VMEM((3, group, width), f32),
        "ym": pltpu.VMEM((group, width), f32),
        "links": pltpu.SMEM((group, pairs, blk), jnp.int32),
        "l_sem": pltpu.SemaphoreType.DMA((5,)),
        "own": pltpu.VMEM((group, 3, ROWS, BLOCK), f32),
        "coord": [pltpu.VMEM((4, SPAN, BLOCK), f32) for _ in range(group)],
        "dual": pltpu.VMEM((group, SPAN, BLOCK), f32),
        "part": pltpu.VMEM((ITERS, group, SPAN, BLOCK), f32),
        "got": pltpu.VMEM((ITERS, group, 2, SPAN, BLOCK), f32),
        "cost": pltpu.VMEM((group, blk, pairs, BLOCK, BLOCK), f32),
        "xcol": pltpu.VMEM((3, blk, BLOCK, BLOCK), f32),
        "acol": pltpu.VMEM((blk, BLOCK, BLOCK), f32),
        "tops": pltpu.VMEM((group, blk, 8, BLOCK), f32),
        "picked": pltpu.VMEM((blk, SPAN, BLOCK), f32),
        "best": pltpu.VMEM((SPAN, BLOCK), f32),
        "acc": pltpu.VMEM((blk, 4, BLOCK, BLOCK), f32),
        "grad": pltpu.VMEM((SPAN, BLOCK), f32),
        "grad_near": pltpu.VMEM((SPAN, BLOCK), f32),
        "grad_far": pltpu.VMEM((peers // CORES, SPAN, BLOCK), f32),
        "c_send": pltpu.SemaphoreType.DMA((group, 2)),
        "c_recv": pltpu.SemaphoreType.DMA((group, 2)),
        "p_send": pltpu.SemaphoreType.DMA((ITERS, group, 4)),
        "p_recv": pltpu.SemaphoreType.DMA((ITERS, group, 4)),
        "n_send": pltpu.SemaphoreType.DMA,
        "n_recv": pltpu.SemaphoreType.DMA,
        "f_send": pltpu.SemaphoreType.DMA((peers // CORES,)),
        "f_recv": pltpu.SemaphoreType.DMA((peers // CORES,)),
    }
    flat, tree = jax.tree.flatten(names)

    def run(*refs):
        kernel(group, blk, pairs, count, peers, refs[:5], refs[5:7], jax.tree.unflatten(tree, refs[7:]))

    whole = pl.BlockSpec(memory_space=pltpu.VMEM)
    held = pl.BlockSpec(memory_space=pltpu.HBM)
    elements = group * blk * pairs * BLOCK * BLOCK
    grad, pots = pl.pallas_call(
        run,
        out_shape=(
            jax.ShapeDtypeStruct((3, width), f32),
            jax.ShapeDtypeStruct((group, width), f32),
        ),
        in_specs=[held] * 5,
        out_specs=(whole, whole),
        scratch_shapes=flat,
        compiler_params=pltpu.CompilerParams(
            collective_id=0, has_side_effects=True, vmem_limit_bytes=63 * 1024 * 1024
        ),
        cost_estimate=pl.CostEstimate(
            flops=40 * elements, bytes_accessed=200000, transcendentals=6 * elements
        ),
        name="sinkhorn",
    )(
        template_points,
        template_mass,
        target_points.transpose(1, 0, 2),
        target_mass,
        pattern.transpose(0, 2, 1),
    )
    return grad, pots


def solution(mesh):
    placed = (
        P(None, "pts"),
        P("pts"),
        P("tgt", None, "pts"),
        P("tgt", "pts"),
        P("tgt", "pts", None),
    )
    return jax.shard_map(
        shards,
        mesh=mesh,
        in_specs=placed,
        out_specs=(P(None, "pts"), P("tgt", "pts")),
        check_vma=False,
    )
```

```python
import functools
import math

import jax
import jax.numpy as jnp
from jax import lax
from jax.experimental import pallas as pl
from jax.experimental.pallas import tpu as pltpu
from jax.sharding import PartitionSpec as P

BLOCK = 128
REACH = 12
ITERS = 3

entropic = 0.02
marginal = 0.5
lowest = -1e30
shrink = marginal / (marginal + entropic)
unit = math.log2(math.e) / entropic

MESH = pl.DeviceIdType.MESH
ROWS = 16
SPAN = 3 * ROWS
OWN = slice(ROWS, 2 * ROWS)
CORES = 2


def kernel(group, blk, pairs, count, peers, refs, outs, scratch):
    grad_ref, pot_ref = outs
    s = scratch
    held = ["yp", "ym", "xp", "xm", "links"]
    order = [2, 3, 0, 1, 4]
    loads = [
        pltpu.make_async_copy(refs[order[i]], s[name], s["l_sem"].at[i]) for i, name in enumerate(held)
    ]
    xp_ref, xm_ref, yp_ref, ym_ref, links_ref = (s[name] for name in ("xp", "xm", "yp", "ym", "links"))
    me = lax.axis_index("pts")
    mine = lax.axis_index("tgt")
    chips = peers // CORES
    chip = mine // CORES
    base = me * blk

    def at_distance(step):
        return {"pts": lax.rem(me + count + step, count)}

    sibling = {"tgt": chip * CORES + 1 - lax.rem(mine, CORES)}

    def same_core(step):
        return {"tgt": lax.rem(mine + step * CORES, peers)}

    greeted = [at_distance(step) for step in (-2, -1, 1, 2)]
    greeted += [sibling] + [same_core(step) for step in range(1, chips)]
    barrier = pltpu.get_barrier_semaphore()
    for other in greeted:
        pl.semaphore_signal(barrier, inc=1, device_id=other, device_id_type=MESH)

    def remote(src, dst, send, recv, to):
        return pltpu.make_async_remote_copy(
            src_ref=src, dst_ref=dst, send_sem=send, recv_sem=recv, device_id=to, device_id_type=MESH
        )

    def coord_copies(t):
        win, send, recv = s["coord"][t], s["c_send"].at[t], s["c_recv"].at[t]
        own = win.at[:, pl.ds(ROWS, ROWS)]
        return [
            remote(own, win.at[:, pl.ds(2 * ROWS, ROWS)], send.at[0], recv.at[0], at_distance(-1)),
            remote(own, win.at[:, pl.ds(0, ROWS)], send.at[1], recv.at[1], at_distance(1)),
        ]

    def part_copies(turn, t):
        part, got = s["part"].at[turn, t], s["got"].at[turn, t]
        send, recv = s["p_send"].at[turn, t], s["p_recv"].at[turn, t]
        lower, upper = pl.ds(0, ROWS), pl.ds(2 * ROWS, ROWS)
        not_lower, not_upper = pl.ds(ROWS, 2 * ROWS), pl.ds(0, 2 * ROWS)
        return [
            remote(part.at[lower], got.at[0, upper], send.at[0], recv.at[0], at_distance(-2)),
            remote(part.at[upper], got.at[1, lower], send.at[1], recv.at[1], at_distance(2)),
            remote(part.at[not_upper], got.at[1, not_lower], send.at[2], recv.at[2], at_distance(-1)),
            remote(part.at[not_lower], got.at[0, not_upper], send.at[3], recv.at[3], at_distance(1)),
        ]

    def start(copies):
        for c in copies:
            c.start()

    def wait_send(copies):
        for c in copies:
            c.wait_send()

    def wait_recv(copies):
        for c in copies:
            c.wait_recv()

    for load in loads:
        load.start()
    loads[0].wait()
    loads[1].wait()
    for t in range(group):
        for q in range(blk):
            lanes = slice(q * BLOCK, (q + 1) * BLOCK)
            for c in range(3):
                row = yp_ref[c, t : t + 1, lanes]
                s["coord"][t][c, ROWS + q : ROWS + q + 1] = row
                s["own"][t, c, q : q + 1] = row
            s["coord"][t][3, ROWS + q : ROWS + q + 1] = jnp.log2(ym_ref[t : t + 1, lanes])
        for c in range(4):
            s["coord"][t][c, ROWS + blk : 2 * ROWS] = jnp.zeros((ROWS - blk, BLOCK), jnp.float32)

    pl.semaphore_wait(barrier, len(greeted))
    for t in range(group):
        start(coord_copies(t))

    for load in loads[2:]:
        load.wait()

    def columns(p, _):
        lanes = pl.ds(pl.multiple_of(p * BLOCK, BLOCK), BLOCK)
        for c in range(3):
            row = xp_ref[c : c + 1, lanes]
            s["xcol"][c, p] = jnp.transpose(jnp.broadcast_to(row, (BLOCK, BLOCK)))
        row = jnp.log2(xm_ref[lanes]).reshape(1, BLOCK)
        s["acol"][p] = jnp.transpose(jnp.broadcast_to(row, (BLOCK, BLOCK)))
        return 0

    lax.fori_loop(0, blk, columns, 0, unroll=2)

    def tile_cost(t, p, k, w):
        y = [s["coord"][t][c, pl.ds(w, 1), :] for c in range(3)]
        for r in range(0, BLOCK, 32):
            d = [s["xcol"][c, p, r : r + 32] - y[c] for c in range(3)]
            total = d[0] * d[0] + d[1] * d[1] + d[2] * d[2]
            s["cost"][t, p, k, r : r + 32] = total * (0.5 * unit)

    def own_tiles(p, _):
        for t in range(group):
            for r in range(0, BLOCK, 32):
                y = [s["own"][t, c, pl.ds(p, 1), :] for c in range(3)]
                d = [s["xcol"][c, p, r : r + 32] - y[c] for c in range(3)]
                total = d[0] * d[0] + d[1] * d[1] + d[2] * d[2]
                s["cost"][t, p, 0, r : r + 32] = total * (0.5 * unit)
        return 0

    lax.fori_loop(0, blk, own_tiles, 0)

    rows_iota = lax.broadcasted_iota(jnp.int32, (SPAN, BLOCK), 0)

    def window_row(t, p, k):
        if k == 0:
            return ROWS + p
        w = jnp.clip(links_ref[t, k, p] - base + REACH, 0, blk + 2 * REACH - 1)
        pad = ROWS - blk
        return w + jnp.where(w >= blk, pad, 0) + jnp.where(w >= 2 * blk, pad, 0)

    def sweep(turn, t):
        first, last = turn == 0, turn == ITERS - 1
        cost = s["cost"]

        def body(p, _):
            where = [window_row(t, p, k) for k in range(pairs)]
            if first:
                duals = [s["coord"][t][3, pl.ds(w, 1), :] for w in where]
                for k in range(1, pairs):
                    tile_cost(t, p, k, where[k])
            else:
                duals = [s["dual"][t, pl.ds(w, 1), :] for w in where]
            heads = []
            for r in range(0, BLOCK, 32):
                costs = [cost[t, p, k, r : r + 32] for k in range(pairs)]
                args = [duals[k] - costs[k] for k in range(pairs)]
                if first:
                    top = -jnp.min(functools.reduce(jnp.minimum, costs), axis=1, keepdims=True)
                else:
                    top = jnp.max(functools.reduce(jnp.maximum, args), axis=1, keepdims=True)
                total = functools.reduce(jnp.add, [jnp.exp2(a - top) for a in args])
                total = jnp.sum(total, axis=1, keepdims=True)
                f = (top + jnp.log2(total)) * (-shrink)
                heads.append(s["acol"][p, r : r + 32] + f)
            head = jnp.concatenate(heads, axis=0)
            terms = []
            for k in range(pairs):
                arg = head - cost[t, p, k]
                top = jnp.max(arg, axis=0, keepdims=True)
                h = jnp.exp2(arg - top)
                if last:
                    cost[t, p, k] = h
                    s["tops"][t, p, k : k + 1] = top
                terms.append(top + jnp.log2(jnp.sum(h, axis=0, keepdims=True)))
            picked = jnp.where(rows_iota == where[0], terms[0], lowest)
            for k in range(1, pairs):
                picked = jnp.where(rows_iota == where[k], terms[k], picked)
            s["picked"][p] = picked
            s["best"][...] = jnp.maximum(s["best"][...], picked)
            return 0

        s["best"][...] = jnp.full((SPAN, BLOCK), lowest, jnp.float32)
        lax.fori_loop(0, blk, body, 0, unroll=6)
        best = s["best"][...]

        def add(p, total):
            return total + jnp.exp2(s["picked"][p] - best)

        total = lax.fori_loop(0, blk, add, jnp.zeros((SPAN, BLOCK), jnp.float32), unroll=True)
        s["part"][turn, t] = best + jnp.log2(total)
        start(part_copies(turn, t))

    def settle(turn, t):
        wait_recv(part_copies(turn, t))
        terms = [s["part"][turn, t], s["got"][turn, t, 0], s["got"][turn, t, 1]]
        top = functools.reduce(jnp.maximum, terms)
        total = functools.reduce(jnp.add, [jnp.exp2(a - top) for a in terms])
        g = (top + jnp.log2(total)) * (-shrink)
        s["dual"][t] = s["coord"][t][3] + g
        if turn == ITERS - 1:
            own = g[OWN] * (1.0 / unit)
            for q in range(blk):
                pot_ref[t : t + 1, q * BLOCK : (q + 1) * BLOCK] = own[q : q + 1]

    def pull(t):
        first, last = t == 0, t == group - 1
        acc = s["acc"]

        def body(p, _):
            where = [window_row(t, p, k) for k in range(pairs)]
            scale, y = [], []
            for k in range(pairs):
                scale.append(jnp.exp2(s["tops"][t, p, k : k + 1] + s["dual"][t, pl.ds(where[k], 1), :]))
                y.append([s["coord"][t][c, pl.ds(where[k], 1), :] for c in range(3)])
            parts = []
            for r in range(0, BLOCK, 32):
                sums = [None] * 4 if first else [acc[p, c, r : r + 32] for c in range(4)]
                for k in range(pairs):
                    plan = s["cost"][t, p, k, r : r + 32] * scale[k]
                    new = [plan * y[k][c] for c in range(3)] + [plan]
                    sums = [b if a is None else a + b for a, b in zip(sums, new)]
                if last:
                    parts.append([s["xcol"][c, p, r : r + 32] * sums[3] - sums[c] for c in range(3)])
                else:
                    for c in range(4):
                        acc[p, c, r : r + 32] = sums[c]
            if last:
                for c in range(3):
                    whole = jnp.transpose(jnp.concatenate([a[c] for a in parts], axis=0))
                    s["grad"][pl.ds(c * ROWS + p, 1), :] = jnp.sum(whole, axis=0, keepdims=True)
            return 0

        lax.fori_loop(0, blk, body, 0, unroll=4)

    for turn in range(ITERS):
        for t in range(group):
            if turn == 0:
                wait_recv(coord_copies(t))
            else:
                settle(turn - 1, t)
            sweep(turn, t)

    s["grad"][...] = jnp.zeros(s["grad"].shape, jnp.float32)
    for t in range(group):
        settle(ITERS - 1, t)
        pull(t)

    near = remote(s["grad"], s["grad_near"], s["n_send"], s["n_recv"], sibling)
    near.start()
    for t in range(group):
        wait_send(coord_copies(t))
        for turn in range(ITERS):
            wait_send(part_copies(turn, t))
    near.wait_recv()
    s["grad_far"][chip] = s["grad"][...] + s["grad_near"][...]

    def far(step, slot):
        return remote(
            s["grad_far"].at[chip], s["grad_far"].at[slot], s["f_send"].at[step - 1], s["f_recv"].at[slot],
            same_core(step),
        )

    for step in range(1, chips):
        far(step, chip).start()
    for step in range(1, chips):
        far(step, lax.rem(chip + step, chips)).wait_recv()
    total = s["grad_far"][0]
    for q in range(1, chips):
        total = total + s["grad_far"][q]
    for c in range(3):
        for q in range(blk):
            grad_ref[c : c + 1, q * BLOCK : (q + 1) * BLOCK] = total[c * ROWS + q : c * ROWS + q + 1]
    near.wait_send()
    for step in range(1, chips):
        far(step, chip).wait_send()


def shards(template_points, template_mass, target_points, target_mass, pattern):
    group, blk, pairs = pattern.shape
    width = blk * BLOCK
    count = lax.axis_size("pts")
    peers = lax.axis_size("tgt")
    f32 = jnp.float32

    names = {
        "xp": pltpu.VMEM((3, width), f32),
        "xm": pltpu.VMEM((width,), f32),
        "yp": pltpu.VMEM((3, group, width), f32),
        "ym": pltpu.VMEM((group, width), f32),
        "links": pltpu.SMEM((group, pairs, blk), jnp.int32),
        "l_sem": pltpu.SemaphoreType.DMA((5,)),
        "own": pltpu.VMEM((group, 3, ROWS, BLOCK), f32),
        "coord": [pltpu.VMEM((4, SPAN, BLOCK), f32) for _ in range(group)],
        "dual": pltpu.VMEM((group, SPAN, BLOCK), f32),
        "part": pltpu.VMEM((ITERS, group, SPAN, BLOCK), f32),
        "got": pltpu.VMEM((ITERS, group, 2, SPAN, BLOCK), f32),
        "cost": pltpu.VMEM((group, blk, pairs, BLOCK, BLOCK), f32),
        "xcol": pltpu.VMEM((3, blk, BLOCK, BLOCK), f32),
        "acol": pltpu.VMEM((blk, BLOCK, BLOCK), f32),
        "tops": pltpu.VMEM((group, blk, 8, BLOCK), f32),
        "picked": pltpu.VMEM((blk, SPAN, BLOCK), f32),
        "best": pltpu.VMEM((SPAN, BLOCK), f32),
        "acc": pltpu.VMEM((blk, 4, BLOCK, BLOCK), f32),
        "grad": pltpu.VMEM((SPAN, BLOCK), f32),
        "grad_near": pltpu.VMEM((SPAN, BLOCK), f32),
        "grad_far": pltpu.VMEM((peers // CORES, SPAN, BLOCK), f32),
        "c_send": pltpu.SemaphoreType.DMA((group, 2)),
        "c_recv": pltpu.SemaphoreType.DMA((group, 2)),
        "p_send": pltpu.SemaphoreType.DMA((ITERS, group, 4)),
        "p_recv": pltpu.SemaphoreType.DMA((ITERS, group, 4)),
        "n_send": pltpu.SemaphoreType.DMA,
        "n_recv": pltpu.SemaphoreType.DMA,
        "f_send": pltpu.SemaphoreType.DMA((peers // CORES,)),
        "f_recv": pltpu.SemaphoreType.DMA((peers // CORES,)),
    }
    flat, tree = jax.tree.flatten(names)

    def run(*refs):
        kernel(group, blk, pairs, count, peers, refs[:5], refs[5:7], jax.tree.unflatten(tree, refs[7:]))

    whole = pl.BlockSpec(memory_space=pltpu.VMEM)
    held = pl.BlockSpec(memory_space=pltpu.HBM)
    elements = group * blk * pairs * BLOCK * BLOCK
    grad, pots = pl.pallas_call(
        run,
        out_shape=(
            jax.ShapeDtypeStruct((3, width), f32),
            jax.ShapeDtypeStruct((group, width), f32),
        ),
        in_specs=[held] * 5,
        out_specs=(whole, whole),
        scratch_shapes=flat,
        compiler_params=pltpu.CompilerParams(
            collective_id=0, has_side_effects=True, vmem_limit_bytes=63 * 1024 * 1024
        ),
        cost_estimate=pl.CostEstimate(
            flops=40 * elements, bytes_accessed=200000, transcendentals=6 * elements
        ),
        name="sinkhorn",
    )(
        template_points,
        template_mass,
        target_points.transpose(1, 0, 2),
        target_mass,
        pattern.transpose(0, 2, 1),
    )
    return grad, pots


def solution(mesh):
    placed = (
        P(None, "pts"),
        P("pts"),
        P("tgt", None, "pts"),
        P("tgt", "pts"),
        P("tgt", "pts", None),
    )
    return jax.shard_map(
        shards,
        mesh=mesh,
        in_specs=placed,
        out_specs=(P(None, "pts"), P("tgt", "pts")),
        check_vma=False,
    )
```
